32 devices in a mesh: dp: 16 (over z, y, core), tensor: 2 (over x).
Axes of the slice: x: 2, y: 2, z: 4, core: 2. Of those that a mesh axis runs over, the one named last changes fastest.
Arguments:
- tokens: bfloat16 [16, 1024, 1152], P('dp', 'tensor'), may hold values from -6 to 6
- cond: bfloat16 [16, 1152], P('dp'), may hold values from -6 to 6
- w_ada: bfloat16 [1152, 6912], P('dp', 'tensor'), may hold values from -0.1875 to 0.1875
- b_ada: bfloat16 [6912], P('tensor'), may hold values from -3 to 3
- w_qkv: bfloat16 [1152, 3456], P('dp', 'tensor'), may hold values from -0.1875 to 0.1875
- b_qv: bfloat16 [16, 144], P('tensor'), may hold values from -2 to 2
- w_proj: bfloat16 [1152, 1152], P('dp', 'tensor'), may hold values from -1.5 to 1.5
- b_proj: bfloat16 [1152], replicated, may hold values from -2 to 2
- w_up: bfloat16 [1152, 4608], P('dp', 'tensor'), may hold values from -0.1875 to 0.1875
- b_up: bfloat16 [4608], P('tensor'), may hold values from -3 to 3
- contracting_matrix: bfloat16 [1152, 4608], P('dp', 'tensor'), may hold values from -0.1875 to 0.1875
- b_down: bfloat16 [1152], replicated, may hold values from -2 to 2
- cotangent: bfloat16 [16, 1024, 1152], P('dp', 'tensor'), may hold values from -6 to 6
Outputs:
- output: bfloat16 [16, 1024, 1152], P('dp', 'tensor')
- grad_tokens: float32 [16, 1024, 1152], P('dp', 'tensor')
- grad_cond: float32 [16, 1152], P('dp')
- grad_w_ada: float32 [1152, 6912], P('dp', 'tensor')
- grad_b_ada: float32 [6912], P('tensor')
- grad_w_qkv: float32 [1152, 3456], P('dp', 'tensor')
- grad_b_qv: float32 [16, 144], P('tensor')
- grad_w_proj: float32 [1152, 1152], P('dp', 'tensor')
- grad_b_proj: float32 [1152], replicated
- grad_w_up: float32 [1152, 4608], P('dp', 'tensor')
- grad_b_up: float32 [4608], P('tensor')
- grad_w_down: float32 [1152, 4608], P('dp', 'tensor')
- down_projection_bias_gradient: float32 [1152], replicated
The draws below stay inside these ranges and needn't reach their ends.
All inputs are finite; a program needn't handle non-finite values.
Results may differ from the reference program's by a relative error of at most 0.0169.
The reference program's roundings to bfloat16 on the way count: a program that leaves them out, or rounds other values in their place, can miss the bound.
Values may be sent and summed in bfloat16 or wider, within the bound.
A program may use at most 256 MiB of HBM per device.

```python
import jax
import jax.numpy as jnp
from jax import lax

D = 1152
HEADS = 16
HEAD_DIM = 72
FF = 4608
SEQ = 1024
LATENTS = 16


def shard_levels(own_key, dims, cuts, low, high):
    gain = 1.0
    for axis_at, shards_of in cuts:
        draws = jax.random.uniform(jax.random.fold_in(jax.random.fold_in(own_key, 6), axis_at), (shards_of,), jnp.float32, low / len(cuts), high / len(cuts))
        gain = gain * jnp.repeat(jnp.exp(draws), dims[axis_at] // shards_of).reshape((-1,) + (1,) * (len(dims) - 1 - axis_at))
    return gain


def gaussian(stream_key, extent, width, bound, pieces=(), dtype=jnp.bfloat16):
    array = jax.random.normal(stream_key, extent, jnp.float32) * width
    if len(pieces) > 0:
        array = shard_levels(stream_key, extent, pieces, -0.22, 0.18) * array
    return jnp.clip(array, min=-bound, max=bound).astype(dtype)


def setup_inputs(seed: int = 0) -> dict:
    arg_keys = jax.random.split(jax.random.key(seed), 14)
    tokens = gaussian(arg_keys[0], (LATENTS, SEQ, D), 1.0, 6.0, ((0, 16), (1, 2)))
    cond = gaussian(arg_keys[1], (LATENTS, D), 1.0, 6.0, ((0, 16),))
    w_ada = gaussian(arg_keys[2], (D, 6 * D), D ** -0.5, 0.1875, ((0, 16), (1, 2)))
    b_ada = gaussian(arg_keys[3], (6 * D,), 0.5, 3.0, ((0, 2),))
    w_qkv = gaussian(arg_keys[4], (D, 3 * D), D ** -0.5, 0.1875, ((0, 16), (1, 2)))
    b_qv = gaussian(arg_keys[5], (HEADS, 2 * HEAD_DIM), 0.3, 2.0, ((0, 2),))
    w_proj = gaussian(arg_keys[6], (D, D), (max(D // 64, 1)) ** -0.5, 1.5, ((0, 16), (1, 2)))
    b_proj = gaussian(arg_keys[7], (D,), 0.3, 2.0)
    w_up = gaussian(arg_keys[8], (D, FF), D ** -0.5, 0.1875, ((0, 16), (1, 2)))
    b_up = gaussian(arg_keys[9], (FF,), 0.5, 3.0, ((0, 2),))
    contracting_matrix = gaussian(arg_keys[10], (D, FF), (FF // 4) ** -0.5, 0.1875, ((0, 16), (1, 2)))
    b_down = gaussian(arg_keys[11], (D,), 0.3, 2.0)
    cotangent = gaussian(arg_keys[12], (LATENTS, SEQ, D), 1.0, 6.0, ((0, 16), (1, 2)))
    return {"tokens": tokens, "cond": cond, "w_ada": w_ada, "b_ada": b_ada, "w_qkv": w_qkv, "b_qv": b_qv, "w_proj": w_proj, "b_proj": b_proj, "w_up": w_up, "b_up": b_up, "contracting_matrix": contracting_matrix, "b_down": b_down, "cotangent": cotangent}


@jax.custom_vjp
def low(v):
    return lax.optimization_barrier(v.astype(jnp.bfloat16)).astype(jnp.float32)

@jax.custom_vjp
def low_back(v):
    return v

def low_keep(v):
    return (low(v), None)

def low_pass(kept, grad):
    return (grad,)

def back_keep(v):
    return (v, None)

def back_low(kept, grad):
    return (low(grad),)
low.defvjp(low_keep, low_pass)
low_back.defvjp(back_keep, back_low)
variance_floor = 1e-06
highest = lax.Precision.HIGHEST

def modulate(field, shift, scale):
    mean_removed = field - lax.optimization_barrier(jnp.mean(field, axis=-1, keepdims=True))
    variance = lax.optimization_barrier(jnp.mean(mean_removed * mean_removed, axis=-1, keepdims=True))
    return mean_removed * lax.rsqrt(variance + variance_floor) * (1.0 + scale) + shift

def latent_layer(field, condition, w_ada, b_ada, w_qkv, b_qv, w_proj, b_proj, w_up, b_up, contracting_matrix, b_down):
    lifted = low(jax.nn.silu(condition))
    modulation = low_back(jnp.dot(lifted, w_ada, precision=highest) + b_ada).reshape(6, D)
    normed_one = low(modulate(field, modulation[0], modulation[1]))
    projected = jnp.dot(normed_one, w_qkv, precision=highest).reshape(SEQ, HEADS, 3, HEAD_DIM)
    bias_heads = b_qv.reshape(HEADS, 2, HEAD_DIM)
    query = low(low_back(projected[:, :, 0] + bias_heads[:, 0]))
    keys_heads = low(low_back(projected[:, :, 1]))
    values_heads = low(low_back(projected[:, :, 2] + bias_heads[:, 1]))
    block = min(512, SEQ)
    count = SEQ // block
    query_blocks = query.reshape(count, block, HEADS, HEAD_DIM)

    def attend(query_block):
        scores = jnp.einsum('qhe,khe->hqk', query_block, keys_heads, precision=highest) * HEAD_DIM ** (-0.5)
        scores = low_back(scores)
        top_score = lax.optimization_barrier(jnp.max(scores, axis=-1, keepdims=True))
        weights = jnp.exp(scores - top_score)
        probs = low(weights / lax.optimization_barrier(jnp.sum(weights, axis=-1, keepdims=True)))
        return jnp.einsum('hqk,khe->qhe', probs, values_heads, precision=highest)
    attention_result_rows = lax.map(jax.checkpoint(attend), query_blocks).reshape(SEQ, D)
    attention_result_rows = low(low_back(attention_result_rows))
    branch_a = low_back(jnp.dot(attention_result_rows, w_proj.T, precision=highest) + b_proj)
    middle_hidden_state = field + modulation[2] * branch_a
    normed_two = low(modulate(middle_hidden_state, modulation[3], modulation[4]))
    pre_up = low_back(jnp.dot(normed_two, w_up, precision=highest) + b_up)
    residual_stream = low(jax.nn.gelu(pre_up, approximate=True))
    branch_f = low_back(jnp.dot(residual_stream, contracting_matrix.T, precision=highest) + b_down)
    return middle_hidden_state + modulation[5] * branch_f

def reference(tokens, cond, w_ada, b_ada, w_qkv, b_qv, w_proj, b_proj, w_up, b_up, contracting_matrix, b_down, cotangent):
    inputs = [arr.astype(jnp.float32) for arr in (tokens, cond, w_ada, b_ada, w_qkv, b_qv, w_proj, b_proj, w_up, b_up, contracting_matrix, b_down)]

    def forward(all_tokens, all_cond, *weights):

        def single_latent(latent_pair):
            return latent_layer(latent_pair[0], latent_pair[1], *weights)
        return lax.map(jax.checkpoint(single_latent), (all_tokens, all_cond))
    result, back_fn = jax.vjp(forward, *inputs)
    grads = back_fn(cotangent.astype(jnp.float32))
    return (result.astype(jnp.bfloat16), grads[0], grads[1], grads[2], grads[3], grads[4], grads[5], grads[6], grads[7], grads[8], grads[9], grads[10], grads[11])
```

```python
import functools

import jax
import jax.numpy as jnp
from jax import lax
from jax.experimental import pallas as pl
from jax.experimental.pallas import tpu as pltpu
from jax.sharding import PartitionSpec as P

HEAD_DIM = 72


variance_floor = 1e-06


def narrow(value):
    return value.astype(jnp.bfloat16)


def modulate(field, shift, scale):
    mean_removed = field - jnp.mean(field, axis=-1, keepdims=True)
    variance = jnp.mean(mean_removed * mean_removed, axis=-1, keepdims=True)
    return mean_removed * lax.rsqrt(variance + variance_floor) * (1.0 + scale) + shift


def gelu_tanh(value):
    return jax.nn.gelu(value, approximate=True)


def shifted(value, peers, step):
    pairs = [(i, (i + step) % peers) for i in range(peers)]
    return lax.ppermute(value, "tensor", pairs)


def spread(value, peers):
    return [value] + [shifted(value, peers, k) for k in range(1, peers)]


def gather_sum(blocks, peers):
    total = blocks[0]
    for k in range(1, peers):
        total = total + shifted(narrow(blocks[k]), peers, -k).astype(jnp.float32)
    return total


def joined(blocks):
    return jnp.concatenate(blocks, axis=0)


def mm(left, right):
    return jnp.dot(left, right, preferred_element_type=jnp.float32)


def mm_nt(left, right):
    return lax.dot_general(left, right, (((1,), (1,)), ((), ())), preferred_element_type=jnp.float32)


def mm_tn(left, right):
    return lax.dot_general(left, right, (((0,), (0,)), ((), ())), preferred_element_type=jnp.float32)


def attend_kernel(scale, rows, q_ref, k_ref, v_ref, o_ref):
    keys = k_ref[0]
    values = v_ref[0]
    for at in range(0, q_ref.shape[1], rows):
        scores = mm_nt(q_ref[0, at : at + rows, :], keys) * scale
        weights = jnp.exp(scores - jnp.max(scores, axis=1, keepdims=True))
        inverse = 1.0 / jnp.sum(weights, axis=1, keepdims=True)
        o_ref[0, at : at + rows, :] = narrow(mm(narrow(weights * inverse), values))


def attend_back_kernel(scale, rows, q_ref, k_ref, v_ref, g_ref, dq_ref, dk_ref, dv_ref):
    keys = k_ref[0]
    values = v_ref[0]
    grad_keys = jnp.zeros(keys.shape, jnp.float32)
    grad_values = jnp.zeros(keys.shape, jnp.float32)
    for at in range(0, q_ref.shape[1], rows):
        query = q_ref[0, at : at + rows, :]
        grad = g_ref[0, at : at + rows, :]
        scores = mm_nt(keys, query) * scale
        weights = jnp.exp(scores - jnp.max(scores, axis=0, keepdims=True))
        probs = weights * (1.0 / jnp.sum(weights, axis=0, keepdims=True))
        grad_probs = mm_nt(values, grad)
        delta = jnp.sum(probs * grad_probs, axis=0, keepdims=True)
        grad_scores = narrow(probs * (grad_probs - delta))
        dq_ref[0, at : at + rows, :] = narrow(mm_tn(grad_scores, keys) * scale)
        grad_keys = grad_keys + mm(grad_scores, query)
        grad_values = grad_values + mm(narrow(probs), grad)
    dk_ref[0] = narrow(grad_keys * scale)
    dv_ref[0] = narrow(grad_values)


def per_head(kernel, outs, flops, *arrays):
    heads, seq, width = arrays[0].shape
    block = pl.BlockSpec((1, seq, width), lambda h: (h, 0, 0))
    shape = jax.ShapeDtypeStruct((heads, seq, width), jnp.bfloat16)
    return pl.pallas_call(
        kernel,
        grid=(heads,),
        in_specs=[block] * len(arrays),
        out_specs=[block] * outs,
        out_shape=[shape] * outs,
        compiler_params=pltpu.CompilerParams(vmem_limit_bytes=48 * 1024 * 1024),
        cost_estimate=pl.CostEstimate(
            flops=flops * heads * seq * seq * 128,
            bytes_accessed=heads * seq * 256 * (len(arrays) + outs),
            transcendentals=heads * seq * seq,
        ),
    )(*arrays)


def scatter_rows(value):
    return lax.psum_scatter(narrow(value), "dp", scatter_dimension=0, tiled=True).astype(
        jnp.float32
    )


def gather_rows(value):
    return lax.all_gather(value, "dp", axis=0, tiled=True)


def on_device(
    peers,
    tokens,
    cond,
    w_ada,
    b_ada,
    w_qkv,
    b_qv,
    w_proj,
    b_proj,
    w_up,
    b_up,
    contracting_matrix,
    b_down,
    cotangent,
):
    width = tokens.shape[2]
    heads_here = b_qv.shape[0]
    local_width = heads_here * HEAD_DIM
    own_rows = w_ada.shape[0]
    parts = width // own_rows
    scale = HEAD_DIM ** (-0.5)
    cond_wide = cond.astype(jnp.float32)
    lifted = narrow(jax.nn.silu(cond_wide))
    lifted_rows = lax.all_to_all(
        lifted.reshape(parts, own_rows), "dp", split_axis=0, concat_axis=0, tiled=True
    )
    mod_terms = lax.all_to_all(
        mm(lifted_rows, w_ada), "dp", split_axis=0, concat_axis=0, tiled=True
    )
    mod_part = jnp.sum(mod_terms, axis=0, keepdims=True) + b_ada.astype(jnp.float32)
    mod_flat = lax.all_gather(mod_part, "tensor", axis=1, tiled=True)
    shift_one, scale_one, gate_one, shift_two, scale_two, gate_two = [
        mod_flat[:, k * width : (k + 1) * width] for k in range(6)
    ]
    qkv_full = gather_rows(w_qkv)
    projection_full = gather_rows(w_proj)
    up_full = gather_rows(w_up)
    down_full = gather_rows(contracting_matrix)

    field = tokens[0].astype(jnp.float32)
    grad_out = cotangent[0].astype(jnp.float32)
    grad_f = narrow(grad_out * gate_two)
    normed_one = narrow(modulate(field, shift_one, scale_one))
    ones = spread(normed_one, peers)
    projected = joined([mm(piece, qkv_full) for piece in ones])
    seq = projected.shape[0]
    bias = b_qv.astype(jnp.float32).reshape(heads_here, 2, HEAD_DIM)
    bias = jnp.stack([bias[:, 0], jnp.zeros_like(bias[:, 0]), bias[:, 1]], axis=1)
    projected = narrow(projected + bias.reshape(1, 3 * local_width))
    by_head = jnp.transpose(projected.reshape(seq, heads_here, 3, HEAD_DIM), (2, 1, 0, 3))
    query_heads, keys_heads, values_heads = (by_head[0], by_head[1], by_head[2])
    rows = min(256, seq)
    (attended,) = per_head(
        functools.partial(attend_kernel, scale, rows), 1, 4, query_heads, keys_heads, values_heads
    )
    attended_rows = jnp.transpose(attended, (1, 0, 2)).reshape(seq, local_width)
    tokens_here = field.shape[0]

    def split(value):
        return [value[k * tokens_here : (k + 1) * tokens_here] for k in range(peers)]

    branch_a = gather_sum(
        [mm_nt(piece, projection_full) for piece in split(attended_rows)], peers
    ) + b_proj.astype(jnp.float32)
    middle = field + gate_one * branch_a
    normed_two = narrow(modulate(middle, shift_two, scale_two))
    twos = spread(normed_two, peers)
    feed_grads = spread(grad_f, peers)
    pre_up = [mm(piece, up_full) + b_up.astype(jnp.float32) for piece in twos]
    hidden = [narrow(gelu_tanh(piece)) for piece in pre_up]
    pre_grads = []
    for piece, grad in zip(pre_up, feed_grads):
        _, gelu_back = jax.vjp(gelu_tanh, piece)
        pre_grads.append(narrow(gelu_back(mm(grad, down_full))[0]))
    pre_gradient = joined(pre_grads)
    down_gradient = mm_tn(joined(feed_grads), joined(hidden))
    up_gradient = mm_tn(joined(twos), pre_gradient)
    branch_f_parts = [mm_nt(piece, down_full) for piece in hidden]
    normed_two_parts = [mm_nt(piece, up_full) for piece in pre_grads]
    down_gradient, up_gradient, normed_two_parts, branch_f_parts = lax.optimization_barrier(
        (narrow(down_gradient), narrow(up_gradient), normed_two_parts, branch_f_parts)
    )
    grad_down_out = scatter_rows(down_gradient)
    grad_up_out = scatter_rows(up_gradient)
    grad_normed_two = gather_sum(normed_two_parts, peers)
    branch_f = gather_sum(branch_f_parts, peers) + b_down.astype(jnp.float32)
    result = middle + gate_two * branch_f
    grad_gate_two = jnp.sum(grad_out * branch_f, axis=0)
    down_bias_grad = jnp.sum(grad_f.astype(jnp.float32), axis=0)
    grad_bup = jnp.sum(pre_gradient.astype(jnp.float32), axis=0)

    _, norm_back_two = jax.vjp(modulate, middle, shift_two, scale_two)
    grad_mid_norm, grad_shift_two, grad_scale_two = norm_back_two(grad_normed_two)
    grad_middle = grad_out + grad_mid_norm
    grad_gate_one = jnp.sum(grad_middle * branch_a, axis=0)
    grad_a = narrow(grad_middle * gate_one)
    grad_bproj = jnp.sum(grad_a.astype(jnp.float32), axis=0)
    a_grads = spread(grad_a, peers)
    grad_attended = joined([narrow(mm(piece, projection_full)) for piece in a_grads])
    grad_proj_out = scatter_rows(mm_tn(joined(a_grads), attended_rows))
    grad_heads = jnp.transpose(grad_attended.reshape(seq, heads_here, HEAD_DIM), (1, 0, 2))
    back = per_head(
        functools.partial(attend_back_kernel, scale, rows),
        3,
        10,
        query_heads,
        keys_heads,
        values_heads,
        grad_heads,
    )
    grad_flat = jnp.transpose(jnp.stack(back, axis=0), (2, 1, 0, 3)).reshape(seq, 3 * local_width)
    column_sums = jnp.sum(grad_flat.astype(jnp.float32), axis=0)
    grad_bqv = column_sums.reshape(heads_here, 3, HEAD_DIM)[:, 0::2].reshape(-1)
    grad_qkv_out = scatter_rows(mm_tn(joined(ones), grad_flat))
    grad_normed_one = gather_sum([mm_nt(piece, qkv_full) for piece in split(grad_flat)], peers)
    _, norm_back_one = jax.vjp(modulate, field, shift_one, scale_one)
    grad_in_norm, grad_shift_one, grad_scale_one = norm_back_one(grad_normed_one)
    grad_tokens = grad_middle + grad_in_norm

    token_sums = jnp.concatenate(
        [
            grad_shift_one[0],
            grad_scale_one[0],
            grad_gate_one,
            grad_shift_two[0],
            grad_scale_two[0],
            grad_gate_two,
            grad_bproj,
            down_bias_grad,
        ]
    )
    token_sums = jnp.sum(lax.all_gather(token_sums, "tensor", axis=0), axis=0)
    columns = w_ada.shape[1]
    grad_mod = narrow(
        lax.dynamic_slice_in_dim(token_sums, lax.axis_index("tensor") * columns, columns)
    )
    small = jnp.concatenate(
        [grad_mod.astype(jnp.float32), token_sums[6 * width :], grad_bqv, grad_bup]
    )
    small = lax.all_gather(small, "dp", axis=0)
    grad_mods = narrow(small[:, :columns])
    sums = jnp.sum(small, axis=0)
    ada_bias_grad = sums[:columns]
    shared = sums[columns : columns + 2 * width].reshape(2, width)
    grad_bqv = sums[columns + 2 * width : columns + 2 * width + grad_bqv.shape[0]]
    grad_bup = sums[columns + 2 * width + grad_bqv.shape[0] :]
    grad_ada_out = mm_tn(lifted_rows, grad_mods)
    grad_lifted = lax.psum(mm_nt(grad_mods, w_ada), "tensor")
    grad_lifted = lax.all_to_all(grad_lifted, "dp", split_axis=0, concat_axis=0, tiled=True)
    _, silu_back = jax.vjp(jax.nn.silu, cond_wide)
    grad_cond = silu_back(grad_lifted.reshape(1, width))[0]
    return (
        narrow(result)[None],
        grad_tokens[None],
        grad_cond,
        grad_ada_out,
        ada_bias_grad,
        grad_qkv_out,
        grad_bqv.reshape(heads_here, 2 * HEAD_DIM),
        grad_proj_out,
        shared[0],
        grad_up_out,
        grad_bup,
        grad_down_out,
        shared[1],
    )


def solution(mesh):
    return jax.shard_map(
        functools.partial(on_device, mesh.shape["tensor"]),
        mesh=mesh,
        in_specs=(
            P("dp", "tensor", None),
            P("dp", None),
            P("dp", "tensor"),
            P("tensor"),
            P("dp", "tensor"),
            P("tensor", None),
            P("dp", "tensor"),
            P(),
            P("dp", "tensor"),
            P("tensor"),
            P("dp", "tensor"),
            P(),
            P("dp", "tensor", None),
        ),
        out_specs=(
            P("dp", "tensor", None),
            P("dp", "tensor", None),
            P("dp", None),
            P("dp", "tensor"),
            P("tensor"),
            P("dp", "tensor"),
            P("tensor", None),
            P("dp", "tensor"),
            P(),
            P("dp", "tensor"),
            P("tensor"),
            P("dp", "tensor"),
            P(),
        ),
        check_vma=False,
    )
```

```python
import functools

import jax
import jax.numpy as jnp
from jax import lax
from jax.experimental import pallas as pl
from jax.experimental.pallas import tpu as pltpu
from jax.sharding import PartitionSpec as P

HEAD_DIM = 72


variance_floor = 1e-06


def narrow(value):
    return value.astype(jnp.bfloat16)


def modulate(field, shift, scale):
    mean_removed = field - jnp.mean(field, axis=-1, keepdims=True)
    variance = jnp.mean(mean_removed * mean_removed, axis=-1, keepdims=True)
    return mean_removed * lax.rsqrt(variance + variance_floor) * (1.0 + scale) + shift


def gelu_tanh(value):
    return jax.nn.gelu(value, approximate=True)


def shifted(value, peers, step):
    pairs = [(i, (i + step) % peers) for i in range(peers)]
    return lax.ppermute(value, "tensor", pairs)


def spread(value, peers):
    return [value] + [shifted(value, peers, k) for k in range(1, peers)]


def gather_sum(blocks, peers):
    total = blocks[0]
    for k in range(1, peers):
        total = total + shifted(narrow(blocks[k]), peers, -k).astype(jnp.float32)
    return total


def joined(blocks):
    return jnp.concatenate(blocks, axis=0)


def mm(left, right):
    return jnp.dot(left, right, preferred_element_type=jnp.float32)


def mm_nt(left, right):
    return lax.dot_general(left, right, (((1,), (1,)), ((), ())), preferred_element_type=jnp.float32)


def mm_tn(left, right):
    return lax.dot_general(left, right, (((0,), (0,)), ((), ())), preferred_element_type=jnp.float32)


def attend_kernel(scale, rows, q_ref, k_ref, v_ref, o_ref):
    keys = k_ref[0]
    values = v_ref[0]
    for at in range(0, q_ref.shape[1], rows):
        scores = mm_nt(q_ref[0, at : at + rows, :], keys) * scale
        weights = jnp.exp(scores - jnp.max(scores, axis=1, keepdims=True))
        inverse = 1.0 / jnp.sum(weights, axis=1, keepdims=True)
        o_ref[0, at : at + rows, :] = narrow(mm(narrow(weights * inverse), values))


def attend_back_kernel(scale, rows, q_ref, k_ref, v_ref, g_ref, dq_ref, dk_ref, dv_ref):
    keys = k_ref[0]
    values = v_ref[0]
    grad_keys = jnp.zeros(keys.shape, jnp.float32)
    grad_values = jnp.zeros(keys.shape, jnp.float32)
    for at in range(0, q_ref.shape[1], rows):
        query = q_ref[0, at : at + rows, :]
        grad = g_ref[0, at : at + rows, :]
        scores = mm_nt(keys, query) * scale
        weights = jnp.exp(scores - jnp.max(scores, axis=0, keepdims=True))
        probs = weights * (1.0 / jnp.sum(weights, axis=0, keepdims=True))
        grad_probs = mm_nt(values, grad)
        delta = jnp.sum(probs * grad_probs, axis=0, keepdims=True)
        grad_scores = narrow(probs * (grad_probs - delta))
        dq_ref[0, at : at + rows, :] = narrow(mm_tn(grad_scores, keys) * scale)
        grad_keys = grad_keys + mm(grad_scores, query)
        grad_values = grad_values + mm(narrow(probs), grad)
    dk_ref[0] = narrow(grad_keys * scale)
    dv_ref[0] = narrow(grad_values)


def per_head(kernel, outs, flops, *arrays):
    heads, seq, width = arrays[0].shape
    seq_keys = arrays[1].shape[1]
    block = pl.BlockSpec((1, seq, width), lambda h: (h, 0, 0))
    shape = jax.ShapeDtypeStruct((heads, seq, width), jnp.bfloat16)
    return pl.pallas_call(
        kernel,
        grid=(heads,),
        in_specs=[pl.BlockSpec((1,) + a.shape[1:], lambda h: (h, 0, 0)) for a in arrays],
        out_specs=[block] * outs,
        out_shape=[shape] * outs,
        compiler_params=pltpu.CompilerParams(vmem_limit_bytes=48 * 1024 * 1024),
        cost_estimate=pl.CostEstimate(
            flops=flops * heads * seq * seq_keys * 256,
            bytes_accessed=heads * seq * 256 * (len(arrays) + outs),
            transcendentals=heads * seq * seq_keys,
        ),
    )(*arrays)


def scatter_rows(value):
    return lax.psum_scatter(narrow(value), "dp", scatter_dimension=0, tiled=True).astype(
        jnp.float32
    )


def gather_rows(value):
    return lax.all_gather(value, "dp", axis=0, tiled=True)


def on_device(
    peers,
    tokens,
    cond,
    w_ada,
    b_ada,
    w_qkv,
    b_qv,
    w_proj,
    b_proj,
    w_up,
    b_up,
    contracting_matrix,
    b_down,
    cotangent,
):
    width = tokens.shape[2]
    heads_here = b_qv.shape[0]
    local_width = heads_here * HEAD_DIM
    own_rows = w_ada.shape[0]
    parts = width // own_rows
    scale = HEAD_DIM ** (-0.5)
    cond_wide = cond.astype(jnp.float32)
    lifted = narrow(jax.nn.silu(cond_wide))
    lifted_rows = lax.all_to_all(
        lifted.reshape(parts, own_rows), "dp", split_axis=0, concat_axis=0, tiled=True
    )
    mod_terms = lax.all_to_all(
        mm(lifted_rows, w_ada), "dp", split_axis=0, concat_axis=0, tiled=True
    )
    mod_part = jnp.sum(mod_terms, axis=0, keepdims=True) + b_ada.astype(jnp.float32)
    mod_flat = lax.all_gather(mod_part, "tensor", axis=1, tiled=True)
    shift_one, scale_one, gate_one, shift_two, scale_two, gate_two = [
        mod_flat[:, k * width : (k + 1) * width] for k in range(6)
    ]
    qkv_full = gather_rows(w_qkv)
    projection_full = gather_rows(w_proj)
    up_full = gather_rows(w_up)
    down_full = gather_rows(contracting_matrix)

    field = tokens[0].astype(jnp.float32)
    grad_out = cotangent[0].astype(jnp.float32)
    grad_f = narrow(grad_out * gate_two)
    normed_one = narrow(modulate(field, shift_one, scale_one))
    ones = spread(normed_one, peers)
    projected = joined([mm(piece, qkv_full) for piece in ones])
    seq = projected.shape[0]
    bias = b_qv.astype(jnp.float32).reshape(heads_here, 2, HEAD_DIM)
    bias = jnp.stack([bias[:, 0], jnp.zeros_like(bias[:, 0]), bias[:, 1]], axis=1)
    projected = narrow(projected + bias.reshape(1, 3 * local_width))
    by_head = jnp.transpose(projected.reshape(seq, heads_here, 3, HEAD_DIM), (2, 1, 0, 3))
    query_heads, keys_heads, values_heads = (by_head[0], by_head[1], by_head[2])
    tokens_here = field.shape[0]
    rows = min(256, tokens_here)
    feed_grads = spread(grad_f, peers)
    query_heads, keys_heads, values_heads, feed_grads = lax.optimization_barrier(
        (query_heads, keys_heads, values_heads, feed_grads)
    )

    def split(value):
        return [value[k * tokens_here : (k + 1) * tokens_here] for k in range(peers)]

    def attend_tokens(k):
        queries = query_heads[:, k * tokens_here : (k + 1) * tokens_here]
        (out,) = per_head(
            functools.partial(attend_kernel, scale, rows), 1, 4, queries, keys_heads, values_heads
        )
        return jnp.transpose(out, (1, 0, 2)).reshape(tokens_here, local_width)

    attended_blocks = [None] * peers
    for k in reversed(range(peers)):
        attended_blocks[k] = attend_tokens(k)
    attended_rows = joined(attended_blocks)
    branch_a = gather_sum(
        [mm_nt(piece, projection_full) for piece in attended_blocks], peers
    ) + b_proj.astype(jnp.float32)
    middle = field + gate_one * branch_a
    normed_two = narrow(modulate(middle, shift_two, scale_two))
    twos = spread(normed_two, peers)
    pre_up = [mm(piece, up_full) + b_up.astype(jnp.float32) for piece in twos]
    hidden = [narrow(gelu_tanh(piece)) for piece in pre_up]
    pre_grads = []
    for piece, grad in zip(pre_up, feed_grads):
        _, gelu_back = jax.vjp(gelu_tanh, piece)
        pre_grads.append(narrow(gelu_back(mm(grad, down_full))[0]))
    pre_gradient = joined(pre_grads)
    down_gradient = mm_tn(joined(feed_grads), joined(hidden))
    up_gradient = mm_tn(joined(twos), pre_gradient)
    branch_f = gather_sum([mm_nt(piece, down_full) for piece in hidden], peers)
    grad_normed_two = gather_sum([mm_nt(piece, up_full) for piece in pre_grads], peers)
    down_gradient = narrow(down_gradient)
    grad_down_out = scatter_rows(down_gradient)
    up_gradient, grad_normed_two, branch_f = lax.optimization_barrier(
        (narrow(up_gradient), grad_normed_two, branch_f)
    )
    branch_f = branch_f + b_down.astype(jnp.float32)
    result = middle + gate_two * branch_f
    grad_gate_two = jnp.sum(grad_out * branch_f, axis=0)
    down_bias_grad = jnp.sum(grad_f.astype(jnp.float32), axis=0)
    grad_bup = jnp.sum(pre_gradient.astype(jnp.float32), axis=0)

    _, norm_back_two = jax.vjp(modulate, middle, shift_two, scale_two)
    grad_mid_norm, grad_shift_two, grad_scale_two = norm_back_two(grad_normed_two)
    grad_middle = grad_out + grad_mid_norm
    grad_gate_one = jnp.sum(grad_middle * branch_a, axis=0)
    grad_a = narrow(grad_middle * gate_one)
    grad_bproj = jnp.sum(grad_a.astype(jnp.float32), axis=0)
    a_grads = spread(grad_a, peers)
    grad_attended = joined([narrow(mm(piece, projection_full)) for piece in a_grads])
    grad_proj_out = scatter_rows(mm_tn(joined(a_grads), attended_rows))
    grad_heads = jnp.transpose(grad_attended.reshape(seq, heads_here, HEAD_DIM), (1, 0, 2))
    grad_heads, grad_down_out, up_gradient = lax.optimization_barrier(
        (grad_heads, grad_down_out, up_gradient)
    )
    grad_up_out = scatter_rows(up_gradient)
    back = per_head(
        functools.partial(attend_back_kernel, scale, rows),
        3,
        10,
        query_heads,
        keys_heads,
        values_heads,
        grad_heads,
    )
    grad_flat = jnp.transpose(jnp.stack(back, axis=0), (2, 1, 0, 3)).reshape(seq, 3 * local_width)
    grad_flat, grad_up_out = lax.optimization_barrier((grad_flat, grad_up_out))
    column_sums = jnp.sum(grad_flat.astype(jnp.float32), axis=0)
    grad_bqv = column_sums.reshape(heads_here, 3, HEAD_DIM)[:, 0::2].reshape(-1)
    grad_qkv_out = scatter_rows(mm_tn(joined(ones), grad_flat))
    grad_normed_one = gather_sum([mm_nt(piece, qkv_full) for piece in split(grad_flat)], peers)
    _, norm_back_one = jax.vjp(modulate, field, shift_one, scale_one)
    grad_in_norm, grad_shift_one, grad_scale_one = norm_back_one(grad_normed_one)
    grad_tokens = grad_middle + grad_in_norm

    token_sums = jnp.concatenate(
        [
            grad_shift_one[0],
            grad_scale_one[0],
            grad_gate_one,
            grad_shift_two[0],
            grad_scale_two[0],
            grad_gate_two,
            grad_bproj,
            down_bias_grad,
        ]
    )
    token_sums = jnp.sum(lax.all_gather(token_sums, "tensor", axis=0), axis=0)
    columns = w_ada.shape[1]
    grad_mod = narrow(
        lax.dynamic_slice_in_dim(token_sums, lax.axis_index("tensor") * columns, columns)
    )
    small = jnp.concatenate(
        [grad_mod.astype(jnp.float32), token_sums[6 * width :], grad_bqv, grad_bup]
    )
    small = lax.all_gather(small, "dp", axis=0)
    grad_mods = narrow(small[:, :columns])
    sums = jnp.sum(small, axis=0)
    ada_bias_grad = sums[:columns]
    shared = sums[columns : columns + 2 * width].reshape(2, width)
    grad_bqv = sums[columns + 2 * width : columns + 2 * width + grad_bqv.shape[0]]
    grad_bup = sums[columns + 2 * width + grad_bqv.shape[0] :]
    grad_ada_out = mm_tn(lifted_rows, grad_mods)
    grad_lifted = lax.psum(mm_nt(grad_mods, w_ada), "tensor")
    grad_lifted = lax.all_to_all(grad_lifted, "dp", split_axis=0, concat_axis=0, tiled=True)
    _, silu_back = jax.vjp(jax.nn.silu, cond_wide)
    grad_cond = silu_back(grad_lifted.reshape(1, width))[0]
    return (
        narrow(result)[None],
        grad_tokens[None],
        grad_cond,
        grad_ada_out,
        ada_bias_grad,
        grad_qkv_out,
        grad_bqv.reshape(heads_here, 2 * HEAD_DIM),
        grad_proj_out,
        shared[0],
        grad_up_out,
        grad_bup,
        grad_down_out,
        shared[1],
    )


def solution(mesh):
    return jax.shard_map(
        functools.partial(on_device, mesh.shape["tensor"]),
        mesh=mesh,
        in_specs=(
            P("dp", "tensor", None),
            P("dp", None),
            P("dp", "tensor"),
            P("tensor"),
            P("dp", "tensor"),
            P("tensor", None),
            P("dp", "tensor"),
            P(),
            P("dp", "tensor"),
            P("tensor"),
            P("dp", "tensor"),
            P(),
            P("dp", "tensor", None),
        ),
        out_specs=(
            P("dp", "tensor", None),
            P("dp", "tensor", None),
            P("dp", None),
            P("dp", "tensor"),
            P("tensor"),
            P("dp", "tensor"),
            P("tensor", None),
            P("dp", "tensor"),
            P(),
            P("dp", "tensor"),
            P("tensor"),
            P("dp", "tensor"),
            P(),
        ),
        check_vma=False,
    )
```
